256 devices in a mesh: patch: 16 (over z_lo, x, core), latent: 16 (over z_hi, y).
Axes of the slice: x: 4, y: 4, z: 8 (z_hi: 4, z_lo: 2; z = z_hi * 2 + z_lo), core: 2. Of those that a mesh axis runs over, the one named last changes fastest.
Arguments:
- queries: bfloat16 [1024, 1536], P('latent', 'patch'), may hold values from -54 to 54
- tile_keys: bfloat16 [12288, 1536], P('patch'), may hold values from -6 to 6
- tile_values: bfloat16 [12288, 1536], P('patch'), may hold values from -6 to 6
- region_ids: int32 [12288], P('patch'), may hold values from 0 to 15
- block_list: int32 [16, 80], P('latent'), may hold values from 0 to 95, as said below
- region_bias: float32 [16, 16], P('latent'), may hold values from -2 to 2
- grad_out: bfloat16 [1024, 1536], P('latent', 'patch'), may hold values from -6 to 6
Outputs:
- attended: bfloat16 [1024, 1536], P('latent', 'patch')
- grad_queries: bfloat16 [1024, 1536], P('latent', 'patch')
- grad_keys: bfloat16 [1536, 12288], P('latent', 'patch')
- grad_values: bfloat16 [1536, 12288], P('latent', 'patch')
The draws below stay inside these ranges and needn't reach their ends.
Inputs may be any that keep to these rules, and one draw needn't show every extreme that they name: `block_list`: each row names 80 different tile blocks.
All inputs are finite; a program needn't handle non-finite values.
Results may differ from the reference program's by a relative error of at most 0.0035.
The reference program's roundings to bfloat16 on the way (of `weights_low` and `dscores`) count: a program that leaves them out, or rounds other values in their place, can miss the bound.
Values may be sent and summed in bfloat16 or wider, within the bound.
No kernel may reach another device: no remote copies, remote signals or barrier semaphores. Data moves between devices by JAX's collectives and lax.ppermute only.
A program may use at most 64 MiB of HBM per device.

```python
import jax
import jax.numpy as jnp
from jax import lax

D = 1536
BLOCK = 128
REGIONS = 16
GROUPS = 16
LATENTS = 1024
NBLOCKS = 96
TILES = 12288
NSEL = 80


def block_choices(key):
    own_key = jax.random.fold_in(key, 7)
    popular = jax.random.randint(jax.random.fold_in(own_key, 1), (NBLOCKS,), 0, 4) == 0
    factor = 1 + 3 * popular.astype(jnp.int32)
    rolled = jax.random.randint(jax.random.fold_in(own_key, 2), (GROUPS, NBLOCKS), 0, 1024)
    ranking = rolled * factor[None, :] * NBLOCKS + jnp.arange(NBLOCKS, dtype=jnp.int32)[None, :]
    unused, picked = lax.top_k(ranking, NSEL)
    return picked.astype(jnp.int32)


def base_keys(key):
    own_key = jax.random.fold_in(key, 11)
    return jnp.clip(jax.random.normal(own_key, (TILES, D), jnp.float32), -6.0, 6.0)


def draw_block_list(key, part):
    return block_choices(key)


def draw_tile_keys(key, part):
    values_drawn = base_keys(key)
    return values_drawn.astype(jnp.bfloat16)


def draw_queries(key, part):
    own_key = jax.random.fold_in(key, 5)
    drawn = jnp.clip(jax.random.normal(own_key, (LATENTS, D), jnp.float32), -6.0, 6.0)
    return drawn.astype(jnp.bfloat16)


def plant(values, key, low, high):
    shape = values.shape
    spot = [jax.random.randint(jax.random.fold_in(key, axis), (), 0, shape[axis]) for axis in range(len(shape))]
    values = values.at[tuple(spot)].set(low)
    longest = shape.index(max(shape))
    spot[longest] = (spot[longest] + 1) % shape[longest]
    return values.at[tuple(spot)].set(high)


def shard_levels(key, shape, cuts, low, largest):
    def one(axis_at, parts):
        steps = jax.random.uniform(jax.random.fold_in(jax.random.fold_in(key, 6), axis_at), (parts,), jnp.float32, low / len(cuts), largest / len(cuts))
        return jnp.repeat(jnp.exp(steps), shape[axis_at] // parts).reshape((-1,) + (1,) * (len(shape) - axis_at - 1))

    factor_of = one(*cuts[0])
    for cut in cuts[1:]:
        factor_of = factor_of * one(*cut)
    return factor_of


def noise(rng, extent, deviation, reach, shards=(), kind=jnp.bfloat16):
    level = shard_levels(rng, extent, shards, -0.22, 0.18) if shards else 1.0
    values = jax.random.normal(rng, extent, jnp.float32) * deviation * level
    return jnp.minimum(jnp.maximum(values, -reach), reach).astype(kind)


def setup_inputs(seed: int = 0) -> dict:
    key_of = jax.random.split(jax.random.key(seed), 8)
    return {
        "queries": draw_queries(jax.random.fold_in(key_of[7], 71), 0),
        "tile_keys": draw_tile_keys(jax.random.fold_in(key_of[7], 71), 0),
        "tile_values": noise(key_of[2], (TILES, D), 1.0, 6.0, ((0, 16),)),
        "region_ids": plant(jax.random.randint(key_of[3], (TILES,), 0, REGIONS), jax.random.fold_in(key_of[3], 1), 0, REGIONS - 1).astype(jnp.int32),
        "block_list": draw_block_list(jax.random.fold_in(key_of[7], 71), 0),
        "region_bias": jnp.clip(jax.random.uniform(key_of[5], (GROUPS, REGIONS), jnp.float32, -2.0, 2.0) * shard_levels(key_of[5], (GROUPS, REGIONS), ((0, 16),), -0.4, 0.0), -2.0, 2.0),
        "grad_out": noise(key_of[6], (LATENTS, D), 1.0, 6.0, ((0, 16), (1, 16))),
    }


def reference(queries, tile_keys, tile_values, region_ids, block_list, region_bias, grad_out):
    feat_width = queries.shape[1]
    score_scale = feat_width ** -0.5
    group_rows = LATENTS // GROUPS
    key_blocks = tile_keys.reshape(NBLOCKS, BLOCK, feat_width)
    value_blocks = tile_values.reshape(NBLOCKS, BLOCK, feat_width)
    region_blocks = region_ids.reshape(NBLOCKS, BLOCK)
    offsets = jnp.arange(BLOCK, dtype=jnp.int32)
    key_grads = jnp.zeros((feat_width, TILES), jnp.float32)
    value_grads = jnp.zeros((feat_width, TILES), jnp.float32)
    attended_parts = []
    query_parts = []
    for group_index in range(GROUPS):
        picked = block_list[group_index]
        key_sel = key_blocks[picked].reshape(-1, feat_width)
        value_sel = value_blocks[picked].reshape(-1, feat_width)
        region_sel = region_blocks[picked].reshape(-1)
        query_rows = queries[group_index * group_rows:(group_index + 1) * group_rows]
        grad_rows = grad_out[group_index * group_rows:(group_index + 1) * group_rows]
        scores = jnp.dot(query_rows, key_sel.T, preferred_element_type=jnp.float32) * score_scale
        scores = scores + region_bias[group_index][region_sel][None, :]
        row_top = jnp.max(scores, axis=1, keepdims=True)
        exp_scores = jnp.exp(scores - row_top)
        weights = exp_scores / jnp.sum(exp_scores, axis=1, keepdims=True)
        weights_low = weights.astype(jnp.bfloat16)
        mixed_rows = jnp.dot(weights_low, value_sel, preferred_element_type=jnp.float32)
        attended_parts.append(mixed_rows.astype(jnp.bfloat16))
        row_delta = jnp.sum(grad_rows.astype(jnp.float32) * mixed_rows, axis=1, keepdims=True)
        dweights = jnp.dot(grad_rows, value_sel.T, preferred_element_type=jnp.float32)
        dscores = (weights * (dweights - row_delta)).astype(jnp.bfloat16)
        query_parts.append((jnp.dot(dscores, key_sel, preferred_element_type=jnp.float32) * score_scale).astype(jnp.bfloat16))
        columns = (picked[:, None].astype(jnp.int32) * BLOCK + offsets[None, :]).reshape(-1).astype(jnp.int32)
        key_grads = key_grads.at[:, columns].add(jnp.dot(query_rows.T, dscores, preferred_element_type=jnp.float32) * score_scale)
        value_grads = value_grads.at[:, columns].add(jnp.dot(grad_rows.T, weights_low, preferred_element_type=jnp.float32))
    return (jnp.concatenate(attended_parts, axis=0), jnp.concatenate(query_parts, axis=0), key_grads.astype(jnp.bfloat16), value_grads.astype(jnp.bfloat16))
```

```python
import jax
import jax.numpy as jnp
from jax import lax
from jax.experimental import pallas as pl
from jax.experimental.pallas import tpu as pltpu
from jax.sharding import Mesh, PartitionSpec as P

BLOCK = 128
D = 1536
TILES = 768
ROWS = 64
FEAT = 96
NB = 6
WIDE = 256
PATCH = ("zlo", "x", "core")
LATENT = ("zhi", "y")
SCALE = D ** (-0.5)
F32 = jnp.float32
BF16 = jnp.bfloat16
NT = (((1,), (1,)), ((), ()))
TN = (((0,), (0,)), ((), ()))
MIB = 1024 * 1024


def iota(shape, dim):
    return lax.broadcasted_iota(jnp.int32, shape, dim)


def pack_kernel(list_ref, bias_ref, q_ref, g_ref, out_ref):
    lane = iota((1, 128), 1)
    mask = jnp.zeros((1, 128), F32)
    for i in range(list_ref.shape[1]):
        mask = jnp.where(lane == list_ref[0, i], 1.0, mask)
    bias = jnp.zeros((1, 128), F32)
    for i in range(16):
        bias = jnp.where(lane == i, bias_ref[0, i], bias)
    high = bias.astype(BF16).astype(F32)
    middle = (bias - high).astype(BF16).astype(F32)
    last = bias - high - middle
    row = iota((16, 128), 0)
    meta = jnp.where(row == 0, mask, jnp.where(row == 1, high, jnp.where(row == 2, middle, jnp.where(row == 3, last, 0.0))))
    meta = meta.astype(BF16)
    for to in range(8):
        out_ref[to, 0:64, 0:96] = q_ref[...]
        out_ref[to, 64:128, 0:96] = g_ref[...]
        out_ref[to, 128:144, :] = meta


def turn_kernel(got_ref, q_ref, g_ref):
    for zlo in range(2):
        rows = pl.ds(zlo * FEAT, FEAT)
        for pair in range(2):
            lanes = pl.ds(pair * 128, 128)
            first, second = (pair * 2) * 2 + zlo, (pair * 2 + 1) * 2 + zlo
            for begin, ref in ((0, q_ref), (64, g_ref)):
                both = jnp.concatenate([got_ref[first, begin : begin + 64, :], got_ref[second, begin : begin + 64, :]], axis=0)
                ref[rows, lanes] = both.T[:FEAT, :]
    for zhi in range(4):
        q_ref[192 + 16 * zhi : 208 + 16 * zhi, 0:128] = got_ref[zhi * 2, 128:144, :]


def load(refs, full_ref, sems, place):
    by_slot = [[], [], [], []]
    for source in range(8):
        for inner in range(4):
            for zlo in range(2):
                slot, row = place(source, inner, zlo)
                copy = pltpu.make_async_copy(
                    refs[source].at[inner, pl.ds(zlo * FEAT, FEAT)],
                    full_ref.at[slot, pl.ds(pl.multiple_of(row, 32), FEAT)],
                    sems.at[source * 8 + inner * 2 + zlo],
                )
                copy.start()
                by_slot[slot].append(copy)
    return by_slot


def score_kernel(ids_ref, *refs):
    q_refs, (meta_ref, key_ref, hot_ref, e_ref, stat_ref, mine_ref, full_ref, sems) = refs[:8], refs[8:]
    x, y, core, latent = ids_ref[0], ids_ref[1], ids_ref[2], ids_ref[3]

    def place(source, inner, zlo):
        at = lax.rem(x + 4 - source % 4, 4)
        side = core if source < 4 else 1 - core
        return inner, ((zlo * 4 + at) * 2 + side) * FEAT

    slots = load(q_refs, full_ref, sems, place)
    group = iota((1, WIDE), 1) // ROWS
    for k in range(4):
        for copy in slots[k]:
            copy.wait()
        at = lax.rem(y + 4 - k, 4)
        parts = []
        for kind in range(4):
            height = 96 if kind == 0 else 16
            part = jnp.zeros((height, WIDE), F32)
            for zhi in range(4):
                column = meta_ref[k, 16 * zhi : 16 * zhi + 16, 0:128].astype(F32).T[:height, kind : kind + 1]
                part = jnp.where(group == zhi, column, part)
            parts.append((part - 1.0) * 1e30 if kind == 0 else part)
        table = jnp.concatenate(parts, axis=0).astype(BF16)
        s = jnp.dot(key_ref[...], full_ref[k], preferred_element_type=F32) * SCALE
        s = s + jnp.dot(hot_ref[...], table, preferred_element_type=F32)
        top = jnp.max(s, axis=0, keepdims=True)
        e = jnp.where(s > -1e29, jnp.exp(s - top), 0.0)
        e_ref[at] = e
        stat_ref[pl.ds(at, 1), :] = top
        stat_ref[pl.ds(4 + at, 1), :] = jnp.sum(e, axis=0, keepdims=True)
        mine_ref[at] = full_ref[k, pl.ds(pl.multiple_of(latent * FEAT, 32), FEAT), :]


def dweight_kernel(ids_ref, *refs):
    g_refs, (value_ref, dw_ref, mine_ref, full_ref, sems) = refs[:8], refs[8:]
    x, y, core, latent = ids_ref[0], ids_ref[1], ids_ref[2], ids_ref[3]

    def place(source, inner, zlo):
        at = lax.rem(x + 4 - inner, 4)
        side = core if source < 4 else 1 - core
        return source % 4, ((zlo * 4 + at) * 2 + side) * FEAT

    slots = load(g_refs, full_ref, sems, place)
    for k in range(4):
        for copy in slots[k]:
            copy.wait()
        at = lax.rem(y + 4 - k, 4)
        dw_ref[at] = jnp.dot(value_ref[...], full_ref[k], preferred_element_type=F32)
        mine_ref[at] = full_ref[k, pl.ds(pl.multiple_of(latent * FEAT, 32), FEAT), :]


def delta_kernel(e_ref, dw_ref, stat_ref, all_ref, delta_ref, factor_ref, low_ref):
    tops = all_ref[:, 0:4, :]
    peak = jnp.max(tops, axis=0)
    whole = jnp.sum(all_ref[:, 4:8, :] * jnp.exp(tops - peak[None]), axis=0)
    factor_ref[...] = jnp.exp(stat_ref[0:4, :] - peak) / whole

    def body(k, _):
        low = (e_ref[k] * factor_ref[pl.ds(k, 1), :]).astype(BF16)
        low_ref[k] = low
        delta_ref[pl.ds(k, 1), :] = jnp.sum(low.astype(F32) * dw_ref[k], axis=0, keepdims=True)
        return 0

    lax.fori_loop(0, 4, body, 0)


def own_rows(ids_ref, values_ref, other_ref):
    y, zhi = ids_ref[1], ids_ref[4]
    lanes = pl.ds(pl.multiple_of(lax.div(zhi, 2) * 128, 128), 128)
    both = lax.dot_general(values_ref[y, :, lanes], other_ref[...], TN, preferred_element_type=F32)
    return jnp.where(lax.rem(zhi, 2) == 1, both[ROWS:], both[:ROWS])


def mixed_kernel(ids_ref, low_ref, value_ref, mine_ref, mixed_ref, gv_ref):
    mixed_ref[...] = own_rows(ids_ref, low_ref, value_ref)
    total = jnp.zeros((FEAT, TILES), F32)
    for k in range(4):
        total = total + lax.dot_general(mine_ref[k], low_ref[k], NT, preferred_element_type=F32)
    gv_ref[...] = total.astype(BF16)


def back_kernel(ids_ref, e_ref, dw_ref, factor_ref, deltas_ref, key_ref, mixed_ref, terms_ref, ds_ref):
    delta = jnp.sum(deltas_ref[...], axis=0)
    for k in range(4):
        w = e_ref[k] * factor_ref[k : k + 1, :]
        ds_ref[k] = (w * (dw_ref[k] - delta[k : k + 1, :])).astype(BF16)
    grads = own_rows(ids_ref, ds_ref, key_ref) * SCALE
    terms_ref[...] = jnp.concatenate([mixed_ref[...], grads], axis=0).T


def grad_key_kernel(mine_ref, ds_ref, gk_ref):
    total = jnp.zeros((FEAT, TILES), F32)
    for k in range(4):
        total = total + lax.dot_general(mine_ref[k], ds_ref[k], NT, preferred_element_type=F32)
    gk_ref[...] = (total * SCALE).astype(BF16)


def last_kernel(terms_ref, attended_ref, gq_ref):
    both = jnp.sum(terms_ref[...], axis=0).T
    attended_ref[...] = both[:ROWS].astype(BF16)
    gq_ref[...] = both[ROWS:].astype(BF16)


def call(kernel, outs, ins, scratch=(), flops=0, moved=0, limit=16):
    vmem = pl.BlockSpec(memory_space=pltpu.VMEM)
    places = {
        "v": vmem,
        "s": pl.BlockSpec(memory_space=pltpu.SMEM),
        "a": pl.BlockSpec(memory_space=pl.ANY),
    }
    return pl.pallas_call(
        kernel,
        out_shape=[jax.ShapeDtypeStruct(shape, kind) for shape, kind in outs],
        in_specs=[places[c] for c in ins],
        out_specs=[vmem] * len(outs),
        scratch_shapes=list(scratch),
        compiler_params=pltpu.CompilerParams(vmem_limit_bytes=limit * MIB),
        cost_estimate=pl.CostEstimate(flops=flops, bytes_accessed=moved, transcendentals=0),
    )


def around(value, axis):
    return [value] + [lax.ppermute(value, axis, [(i, (i + k) % 4) for i in range(4)]) for k in (1, 2, 3)]


def swap(value):
    return lax.ppermute(value, "core", [(0, 1), (1, 0)])


def spread(value, axis, size):
    return lax.all_to_all(jnp.broadcast_to(value[None], (size,) + value.shape), axis, 0, 0)


def shards(queries, tile_keys, tile_values, region_ids, block_list, region_bias, grad_out):
    patch = lax.axis_index(PATCH)
    ids = jnp.stack([lax.axis_index(n) for n in ("x", "y", "core")] + [lax.axis_index(LATENT), lax.axis_index("zhi")])
    ids = ids.astype(jnp.int32)

    packed = call(pack_kernel, [((8, 144, 128), BF16)], "ssvv")(block_list, region_bias, queries, grad_out)[0]
    got = lax.all_to_all(packed, ("zhi", "zlo"), 0, 0)
    q_block, g_block = call(turn_kernel, [((256, WIDE), BF16), ((192, WIDE), BF16)], "v")(got)

    q_row = jnp.stack(around(q_block, "y"))
    g_row = jnp.stack(around(g_block, "x"))
    q_all = around(q_row[:, :192], "x")
    g_all = around(g_row, "y")
    q_all = q_all + [swap(part) for part in q_all]
    g_all = g_all + [swap(part) for part in g_all]

    labels = jnp.arange(144, dtype=jnp.int32)[None, :]
    block_at = patch * NB + jnp.arange(TILES, dtype=jnp.int32)[:, None] // BLOCK
    hot = (labels == block_at) | ((labels >= 96) & (labels % 16 == region_ids[:, None]))
    hot = hot.astype(BF16)

    wide = (4, TILES, WIDE)
    full = [pltpu.VMEM((4, D, WIDE), BF16), pltpu.SemaphoreType.DMA((64,))]
    flops = 2 * TILES * 1024 * D
    e, stat, q_mine = call(
        score_kernel,
        [(wide, F32), ((8, WIDE), F32), ((4, FEAT, WIDE), BF16)],
        "s" + "a" * 8 + "vvv",
        full,
        flops,
        10_000_000,
        24,
    )(ids, *q_all, q_row[:, 192:], tile_keys, hot)
    stats = spread(stat, PATCH, 16)
    dw, g_mine = call(
        dweight_kernel,
        [(wide, F32), ((4, FEAT, WIDE), BF16)],
        "s" + "a" * 8 + "v",
        full,
        flops,
        10_000_000,
        24,
    )(ids, *g_all, tile_values)
    delta, factor, low = call(
        delta_kernel, [((4, WIDE), F32), ((4, WIDE), F32), (wide, BF16)], "vvvv", (), 4 * TILES * 1024, 8_000_000
    )(e, dw, stat, stats)
    deltas = spread(delta, PATCH, 16)
    mixed, grad_values = call(
        mixed_kernel,
        [((ROWS, D), F32), ((FEAT, TILES), BF16)],
        "svvv",
        (),
        2 * TILES * 1024 * FEAT,
        5_000_000,
    )(ids, low, tile_values, g_mine)
    terms, ds = call(
        back_kernel, [((D, 128), F32), (wide, BF16)], "svvvvvv", (), 4 * TILES * 128 * D, 10_000_000
    )(ids, e, dw, factor, deltas, tile_keys, mixed)
    sums = lax.all_to_all(terms.reshape(16, FEAT, 128), PATCH, 0, 0)
    (grad_keys,) = call(
        grad_key_kernel, [((FEAT, TILES), BF16)], "vv", (), 2 * TILES * 1024 * FEAT, 2_000_000
    )(q_mine, ds)
    attended, grad_queries = call(last_kernel, [((ROWS, FEAT), BF16)] * 2, "v")(sums)
    return (attended, grad_queries, grad_keys, grad_values)


def solution(mesh):
    fine = Mesh(mesh.devices.reshape(2, 4, 2, 4, 4), PATCH + LATENT)
    in_specs = (
        P(LATENT, PATCH),
        P(PATCH, None),
        P(PATCH, None),
        P(PATCH),
        P(LATENT, None),
        P(LATENT, None),
        P(LATENT, PATCH),
    )
    out_specs = (P(LATENT, PATCH),) * 4
    return jax.shard_map(shards, mesh=fine, in_specs=in_specs, out_specs=out_specs, check_vma=False)
```

```python
import jax
import jax.numpy as jnp
from jax import lax
from jax.experimental import pallas as pl
from jax.experimental.pallas import tpu as pltpu
from jax.sharding import Mesh, PartitionSpec as P

BLOCK = 128
D = 1536
TILES = 768
ROWS = 64
FEAT = 96
NB = 6
WIDE = 256
PART = 384
HIGH = 400
PATCH = ("zlo", "x", "core")
LATENT = ("zhi", "y")
SCALE = D ** (-0.5)
F32 = jnp.float32
BF16 = jnp.bfloat16
NT = (((1,), (1,)), ((), ()))
TN = (((0,), (0,)), ((), ()))
MIB = 1024 * 1024


def iota(shape, dim):
    return lax.broadcasted_iota(jnp.int32, shape, dim)


def pack_kernel(list_ref, bias_ref, q_ref, g_ref, out_ref, list_s, bias_s, q_v, g_v, sems):
    copies = [
        pltpu.make_async_copy(src, dst, sems.at[i])
        for i, (src, dst) in enumerate(((list_ref, list_s), (bias_ref, bias_s), (q_ref, q_v), (g_ref, g_v)))
    ]
    for copy in copies:
        copy.start()
    for copy in copies:
        copy.wait()
    lane = iota((1, 128), 1)
    mask = jnp.zeros((1, 128), F32)
    for i in range(list_ref.shape[1]):
        mask = jnp.where(lane == list_s[0, i], 1.0, mask)
    bias = jnp.zeros((1, 128), F32)
    for i in range(16):
        bias = jnp.where(lane == i, bias_s[0, i], bias)
    high = bias.astype(BF16).astype(F32)
    middle = (bias - high).astype(BF16).astype(F32)
    last = bias - high - middle
    kind = iota((16, 128), 0) % 4
    meta = jnp.where(kind == 0, mask, jnp.where(kind == 1, high, jnp.where(kind == 2, middle, last)))
    meta = meta.astype(BF16)
    for to in range(16):
        out_ref[to, 0:64, 0:96] = q_v[...] if to % 2 == 0 else g_v[...]
        out_ref[to, 64:80, :] = meta


def turn_kernel(got_ref, out_ref):
    for part in range(4):
        for pair in range(2):
            both = jnp.concatenate([got_ref[pair * 8 + part, 0:64, :], got_ref[pair * 8 + 4 + part, 0:64, :]], axis=0)
            out_ref[part * FEAT : part * FEAT + FEAT, pair * 128 : pair * 128 + 128] = both.T[:FEAT, :]
    owner = iota((16, 128), 0) // 4
    meta = jnp.zeros((16, 128), F32)
    for zhi in range(4):
        meta = jnp.where(owner == zhi, got_ref[zhi * 4, 64:80, :].astype(F32), meta)
    out_ref[PART:HIGH, 0:128] = meta.astype(BF16)
    out_ref[PART:HIGH, 128:256] = meta.astype(BF16)


def stack_kernel(*refs):
    for k in range(4):
        refs[4][k] = refs[k][...]


def prepare_kernel(ids_ref, key_ref, value_ref, region_ref, key_out, value_out, hot_ref, sems):
    copies = [
        pltpu.make_async_copy(key_ref, key_out, sems.at[0]),
        pltpu.make_async_copy(value_ref, value_out, sems.at[1]),
    ]
    for copy in copies:
        copy.start()
    for block in range(NB):
        label = iota((256, BLOCK), 0)
        region = region_ref[:, block * BLOCK : (block + 1) * BLOCK]
        at = ids_ref[5] * NB + block
        hot = (label == at) | ((label >= 96) & (label < 144) & (label % 16 == region))
        hot_ref[block * BLOCK : (block + 1) * BLOCK, :] = jnp.where(hot, 1.0, 0.0).T.astype(BF16)
    for copy in copies:
        copy.wait()


def load(refs, full_ref, sems, first, place):
    by_slot = [[], [], [], []]
    for step in range(4):
        for inner in range(4):
            for zlo in range(2):
                slot, at = place(step, inner)
                row = pl.multiple_of((zlo * 4 + at) * 2 * FEAT, 64)
                copies = [
                    pltpu.make_async_copy(
                        refs[step + half].at[inner, pl.ds(zlo * 2 * FEAT, 2 * FEAT)],
                        full_ref.at[slot, pl.ds(row, 2 * FEAT)],
                        sems.at[step * 8 + inner * 2 + zlo],
                    )
                    for half in (0, 4)
                ]
                pl.when(first)(copies[0].start)
                pl.when(jnp.logical_not(first))(copies[1].start)
                by_slot[slot].append(copies[0])
    return by_slot


def score_kernel(ids_ref, *refs):
    q_refs, (key_ref, hot_ref, e_ref, stat_ref, mine_ref, full_ref, meta_ref, sems) = refs[:8], refs[8:]
    x, y, core, latent = ids_ref[0], ids_ref[1], ids_ref[2], ids_ref[3]
    slots = load(q_refs, full_ref, sems, core == 0, lambda step, inner: (inner, lax.rem(x + 4 - step, 4)))
    metas = [pltpu.make_async_copy(q_refs[half].at[:, pl.ds(PART, 16)], meta_ref, sems.at[32]) for half in (0, 4)]
    pl.when(core == 0)(metas[0].start)
    pl.when(core != 0)(metas[1].start)
    metas[0].wait()
    group = iota((1, WIDE), 1) // ROWS
    for k in range(4):
        at = lax.rem(y + 4 - k, 4)
        meta = meta_ref[k, :, 0:128].astype(F32).T
        parts = []
        for kind in range(4):
            height = 96 if kind == 0 else 16
            part = jnp.zeros((height, WIDE), F32)
            for zhi in range(4):
                part = jnp.where(group == zhi, meta[:height, zhi * 4 + kind : zhi * 4 + kind + 1], part)
            parts.append((part - 1.0) * 1e30 if kind == 0 else part)
        table = jnp.concatenate(parts + [jnp.zeros((112, WIDE), F32)], axis=0).astype(BF16)
        for copy in slots[k]:
            copy.wait()
        s = jnp.dot(key_ref[...], full_ref[k], preferred_element_type=F32) * SCALE
        s = s + jnp.dot(hot_ref[...], table, preferred_element_type=F32)
        top = jnp.max(s, axis=0, keepdims=True)
        e = jnp.where(s > -1e29, jnp.exp(s - top), 0.0)
        e_ref[at] = e
        total = jnp.sum(e, axis=0, keepdims=True)
        for to in range(16):
            stat_ref[to, pl.ds(at, 1), :] = top
            stat_ref[to, pl.ds(4 + at, 1), :] = total
        mine_ref[at] = full_ref[k, pl.ds(pl.multiple_of(latent * FEAT, 32), FEAT), :]


def dweight_kernel(ids_ref, *refs):
    g_refs, (value_ref, dw_ref, mine_ref, full_ref, sems) = refs[:8], refs[8:]
    x, y, core, latent = ids_ref[0], ids_ref[1], ids_ref[2], ids_ref[3]
    slots = load(g_refs, full_ref, sems, core == 1, lambda step, inner: (step, lax.rem(x + 4 - inner, 4)))
    for k in range(4):
        for copy in slots[k]:
            copy.wait()
        at = lax.rem(y + 4 - k, 4)
        dw_ref[at] = jnp.dot(value_ref[...], full_ref[k], preferred_element_type=F32)
        mine_ref[at] = full_ref[k, pl.ds(pl.multiple_of(latent * FEAT, 32), FEAT), :]


def delta_kernel(e_ref, dw_ref, stat_ref, all_ref, delta_ref, factor_ref, low_ref):
    tops = all_ref[:, 0:4, :]
    peak = jnp.max(tops, axis=0)
    whole = jnp.sum(all_ref[:, 4:8, :] * jnp.exp(tops - peak[None]), axis=0)
    factor_ref[...] = jnp.exp(stat_ref[0, 0:4, :] - peak) / whole

    def body(k, _):
        low = (e_ref[k] * factor_ref[pl.ds(k, 1), :]).astype(BF16)
        low_ref[k] = low
        delta = jnp.sum(low.astype(F32) * dw_ref[k], axis=0, keepdims=True)
        for to in range(16):
            delta_ref[to, pl.ds(k, 1), :] = delta
        return 0

    lax.fori_loop(0, 4, body, 0)


def own_rows(ids_ref, values_ref, other_ref):
    y, zhi = ids_ref[1], ids_ref[4]
    lanes = pl.ds(pl.multiple_of(lax.div(zhi, 2) * 128, 128), 128)
    both = lax.dot_general(values_ref[y, :, lanes], other_ref[...], TN, preferred_element_type=F32)
    return jnp.where(lax.rem(zhi, 2) == 1, both[ROWS:], both[:ROWS])


def mixed_kernel(ids_ref, low_ref, value_ref, mine_ref, mixed_ref, gv_ref):
    mixed_ref[...] = own_rows(ids_ref, low_ref, value_ref)
    total = jnp.zeros((FEAT, TILES), F32)
    for k in range(4):
        total = total + lax.dot_general(mine_ref[k], low_ref[k], NT, preferred_element_type=F32)
    gv_ref[...] = total.astype(BF16)


def back_kernel(ids_ref, e_ref, dw_ref, factor_ref, deltas_ref, key_ref, mixed_ref, terms_ref, ds_ref):
    delta = jnp.sum(deltas_ref[...], axis=0)
    for k in range(4):
        w = e_ref[k] * factor_ref[k : k + 1, :]
        ds_ref[k] = (w * (dw_ref[k] - delta[k : k + 1, :])).astype(BF16)
    grads = own_rows(ids_ref, ds_ref, key_ref) * SCALE
    terms_ref[...] = jnp.concatenate([mixed_ref[...], grads], axis=0).T


def grad_key_kernel(mine_ref, ds_ref, gk_ref):
    total = jnp.zeros((FEAT, TILES), F32)
    for k in range(4):
        total = total + lax.dot_general(mine_ref[k], ds_ref[k], NT, preferred_element_type=F32)
    gk_ref[...] = (total * SCALE).astype(BF16)


def last_kernel(terms_ref, attended_ref, gq_ref):
    both = jnp.sum(terms_ref[...], axis=0).T
    attended_ref[...] = both[:ROWS].astype(BF16)
    gq_ref[...] = both[ROWS:].astype(BF16)


def call(kernel, outs, ins, args, scratch=(), flops=0, moved=0, limit=16):
    vmem = pl.BlockSpec(memory_space=pltpu.VMEM)
    specs = {"v": vmem, "V": vmem, "s": pl.BlockSpec(memory_space=pltpu.SMEM), "H": pl.BlockSpec(memory_space=pl.ANY)}
    pins = {"V": pltpu.VMEM, "H": pltpu.HBM}
    shapes = [pltpu.VMEM(shape, kind) if c == "V" else jax.ShapeDtypeStruct(shape, kind) for c, shape, kind in outs]
    args = [pltpu.with_memory_space_constraint(a, pins[c]) if c in pins else a for c, a in zip(ins, args)]
    return pl.pallas_call(
        kernel,
        out_shape=shapes,
        in_specs=[specs[c] for c in ins],
        out_specs=[vmem] * len(outs),
        scratch_shapes=list(scratch),
        compiler_params=pltpu.CompilerParams(vmem_limit_bytes=limit * MIB),
        cost_estimate=pl.CostEstimate(flops=flops, bytes_accessed=moved, transcendentals=0),
    )(*args)


PLANE = [(x, core, y) for x in range(4) for core in range(2) for y in range(4)]


def along(value, stage, step):
    pairs = []
    for i, (x, core, y) in enumerate(PLANE):
        to = (x, core, (y + step) % 4) if core == stage else ((x + step) % 4, core, y)
        pairs.append((i, PLANE.index(to)))
    return lax.ppermute(value, ("x", "core", "y"), pairs)


def swap(value):
    return lax.ppermute(value, "core", [(0, 1), (1, 0)])


def shards(queries, tile_keys, tile_values, region_ids, block_list, region_bias, grad_out):
    ids = [lax.axis_index(n) for n in ("x", "y", "core", LATENT, "zhi", PATCH)]
    ids = jnp.stack(ids).astype(jnp.int32)
    dma = pltpu.SemaphoreType.DMA
    wide = (4, TILES, WIDE)
    slices = (4, FEAT, WIDE)

    (packed,) = call(
        pack_kernel,
        [("v", (16, 80, 128), BF16)],
        "HHHH",
        (block_list, region_bias, queries, grad_out),
        [
            pltpu.SMEM(block_list.shape, jnp.int32),
            pltpu.SMEM(region_bias.shape, F32),
            pltpu.VMEM((ROWS, FEAT), BF16),
            pltpu.VMEM((ROWS, FEAT), BF16),
            dma((4,)),
        ],
    )
    got = lax.all_to_all(packed, ("zhi", "zlo", "core"), 0, 0)
    key_in, value_in, hot = call(
        prepare_kernel,
        [("V", (TILES, D), BF16), ("V", (TILES, D), BF16), ("V", (TILES, 256), BF16)],
        "sHHv",
        (ids, tile_keys, tile_values, region_ids.reshape(1, TILES)),
        [dma((2,))],
        0,
        10_000_000,
    )
    (block,) = call(turn_kernel, [("v", (HIGH, WIDE), BF16)], "v", (got,))
    (line,) = call(
        stack_kernel,
        [("v", (4, HIGH, WIDE), BF16)],
        "vvvv",
        [block] + [along(block, 0, k) for k in (1, 2, 3)],
    )
    near = [line] + [along(line, 1, k) for k in (1, 2, 3)]
    planes = near + [swap(part) for part in near]

    full = [pltpu.VMEM((4, D, WIDE), BF16)]
    flops = 2 * TILES * 1024 * D
    e, stat, q_mine = call(
        score_kernel,
        [("V", wide, F32), ("v", (16, 8, WIDE), F32), ("V", slices, BF16)],
        "s" + "H" * 8 + "VV",
        (ids, *planes, key_in, hot),
        full + [pltpu.VMEM((4, 16, WIDE), BF16), dma((33,))],
        flops,
        10_000_000,
    )
    stats = lax.all_to_all(stat, PATCH, 0, 0)
    dw, g_mine = call(
        dweight_kernel,
        [("V", wide, F32), ("V", slices, BF16)],
        "s" + "H" * 8 + "V",
        (ids, *planes, value_in),
        full + [dma((32,))],
        flops,
        10_000_000,
    )
    delta, factor, low = call(
        delta_kernel,
        [("v", (16, 4, WIDE), F32), ("V", (4, WIDE), F32), ("V", wide, BF16)],
        "VVvv",
        (e, dw, stat, stats),
        (),
        4 * TILES * 1024,
        8_000_000,
    )
    deltas = lax.all_to_all(delta, PATCH, 0, 0)
    mixed, grad_values = call(
        mixed_kernel,
        [("V", (ROWS, D), F32), ("v", (FEAT, TILES), BF16)],
        "sVVV",
        (ids, low, value_in, g_mine),
        (),
        2 * TILES * 1024 * FEAT,
        5_000_000,
    )
    terms, ds = call(
        back_kernel,
        [("v", (D, 128), F32), ("V", wide, BF16)],
        "sVVVvVV",
        (ids, e, dw, factor, deltas, key_in, mixed),
        (),
        4 * TILES * 128 * D,
        10_000_000,
    )
    sums = lax.all_to_all(terms.reshape(16, FEAT, 128), PATCH, 0, 0)
    (grad_keys,) = call(
        grad_key_kernel,
        [("v", (FEAT, TILES), BF16)],
        "VV",
        (q_mine, ds),
        (),
        2 * TILES * 1024 * FEAT,
        2_000_000,
    )
    attended, grad_queries = call(last_kernel, [("v", (ROWS, FEAT), BF16)] * 2, "v", (sums,))
    return (attended, grad_queries, grad_keys, grad_values)


def solution(mesh):
    fine = Mesh(mesh.devices.reshape(2, 4, 2, 4, 4), PATCH + LATENT)
    in_specs = (
        P(LATENT, PATCH),
        P(PATCH, None),
        P(PATCH, None),
        P(PATCH),
        P(LATENT, None),
        P(LATENT, None),
        P(LATENT, PATCH),
    )
    out_specs = (P(LATENT, PATCH),) * 4
    return jax.shard_map(shards, mesh=fine, in_specs=in_specs, out_specs=out_specs, check_vma=False)
```

```python
import functools

import jax
import jax.numpy as jnp
from jax import lax
from jax.experimental import pallas as pl
from jax.experimental.pallas import tpu as pltpu
from jax.sharding import Mesh, PartitionSpec as P

BLOCK = 128
D = 1536
TILES = 768
ROWS = 64
FEAT = 96
NB = 6
WIDE = 256
PART = 384
HIGH = 400
PATCH = ("zlo", "x", "core")
LATENT = ("zhi", "y")
SCALE = D ** (-0.5)
F32 = jnp.float32
BF16 = jnp.bfloat16
NT = (((1,), (1,)), ((), ()))
TN = (((0,), (0,)), ((), ()))
MIB = 1024 * 1024


def iota(shape, dim):
    return lax.broadcasted_iota(jnp.int32, shape, dim)


def pack_kernel(list_ref, bias_ref, q_ref, g_ref, out_ref, list_s, bias_s, q_v, g_v, sems):
    copies = [
        pltpu.make_async_copy(src, dst, sems.at[i])
        for i, (src, dst) in enumerate(((list_ref, list_s), (bias_ref, bias_s), (q_ref, q_v), (g_ref, g_v)))
    ]
    for copy in copies:
        copy.start()
    for copy in copies:
        copy.wait()
    lane = iota((1, 128), 1)
    mask = jnp.zeros((1, 128), F32)
    for i in range(list_ref.shape[1]):
        mask = jnp.where(lane == list_s[0, i], 1.0, mask)
    bias = jnp.zeros((1, 128), F32)
    for i in range(16):
        bias = jnp.where(lane == i, bias_s[0, i], bias)
    high = bias.astype(BF16).astype(F32)
    middle = (bias - high).astype(BF16).astype(F32)
    last = bias - high - middle
    kind = iota((16, 128), 0) % 4
    meta = jnp.where(kind == 0, mask, jnp.where(kind == 1, high, jnp.where(kind == 2, middle, last)))
    meta = meta.astype(BF16)
    for to in range(16):
        out_ref[to, 0:64, 0:96] = q_v[...] if to % 2 == 0 else g_v[...]
        out_ref[to, 64:80, :] = meta


def turn_kernel(got_ref, out_ref):
    for part in range(4):
        for pair in range(2):
            both = jnp.concatenate([got_ref[pair * 8 + part, 0:64, :], got_ref[pair * 8 + 4 + part, 0:64, :]], axis=0)
            out_ref[part * FEAT : part * FEAT + FEAT, pair * 128 : pair * 128 + 128] = both.T[:FEAT, :]
    owner = iota((16, 128), 0) // 4
    meta = jnp.zeros((16, 128), F32)
    for zhi in range(4):
        meta = jnp.where(owner == zhi, got_ref[zhi * 4, 64:80, :].astype(F32), meta)
    out_ref[PART:HIGH, 0:128] = meta.astype(BF16)
    out_ref[PART:HIGH, 128:256] = meta.astype(BF16)


def stack_kernel(*refs):
    for k in range(4):
        refs[5 + k // 2][k % 2] = refs[k][...]


def tie_kernel(*refs):
    pass


def add_kernel(first_ref, second_ref, out_ref):
    out_ref[...] = first_ref[...] + second_ref[...]


def prepare_kernel(key_ref, value_ref, region_ref, key_out, value_out, hot_ref, key_v, value_v, sems):
    copies = [
        pltpu.make_async_copy(key_ref, key_v, sems.at[0]),
        pltpu.make_async_copy(value_ref, value_v, sems.at[1]),
    ]
    for copy in copies:
        copy.start()
    for block in range(NB):
        label = iota((256, BLOCK), 0)
        region = region_ref[:, block * BLOCK : (block + 1) * BLOCK]
        at = lax.axis_index(PATCH) * NB + block
        hot = (label == at) | ((label >= 96) & (label < 144) & (label % 16 == region))
        hot_ref[block * BLOCK : (block + 1) * BLOCK, :] = jnp.where(hot, 1.0, 0.0).T.astype(BF16)
    for copy, src, dst in zip(copies, (key_v, value_v), (key_out, value_out)):
        copy.wait()
        for x in range(4):
            low = src[:, x * 192 : x * 192 + 192]
            high = src[:, (4 + x) * 192 : (4 + x) * 192 + 192]
            dst[x] = jnp.concatenate([low, high], axis=1)


def place(back):
    return lax.rem(lax.axis_index("x") + 4 - back, 4), lax.rem(lax.axis_index("y") + 4 - back, 4)


def part(step, q_refs, g_refs, key_ref, value_ref, s_in, s_ref, dw_ref):
    x_at, y_at = place(step)
    total = jnp.zeros((TILES, WIDE), F32)
    for k in range(4):
        at = place(k)[1]
        term = jnp.dot(key_ref[x_at], q_refs[k // 2][k % 2, 0:PART, :], preferred_element_type=F32)
        s_ref[at] = term if s_in is None else s_in[at] + term
        total = total + jnp.dot(value_ref[place(k)[0]], g_refs[k // 2][k % 2, 0:PART, :], preferred_element_type=F32)
    dw_ref[y_at] = total


def by_core(body, planes):
    core = lax.axis_index("core")
    pl.when(core == 0)(lambda: body(planes[:2], planes[2:]))
    pl.when(core == 1)(lambda: body(planes[2:], planes[:2]))


def first_kernel(*refs):
    planes, (key_ref, value_ref, s_ref, dw_ref, table_ref) = refs[:4], refs[4:]
    group = iota((1, WIDE), 1) // ROWS

    def body(q_refs, g_refs):
        for k in range(4):
            meta = q_refs[k // 2][k % 2, PART:HIGH, 0:128].astype(F32).T
            parts = []
            for kind in range(4):
                height = 96 if kind == 0 else 16
                piece = jnp.zeros((height, WIDE), F32)
                for zhi in range(4):
                    piece = jnp.where(group == zhi, meta[:height, zhi * 4 + kind : zhi * 4 + kind + 1], piece)
                parts.append((piece - 1.0) * 1e30 if kind == 0 else piece)
            table = jnp.concatenate(parts + [jnp.zeros((112, WIDE), F32)], axis=0)
            table_ref[place(k)[1]] = table.astype(BF16)
        part(0, q_refs, g_refs, key_ref, value_ref, None, s_ref, dw_ref)

    by_core(body, planes)


def middle_kernel(step, *refs):
    planes, (key_ref, value_ref, s_in, dw_in, s_ref, dw_ref) = refs[:4], refs[4:]
    by_core(lambda q, g: part(step, q, g, key_ref, value_ref, s_in, s_ref, dw_ref), planes)


def end_kernel(*refs):
    planes, (key_ref, value_ref, table_ref, hot_ref, s_in, dw_in, s_ref, dw_ref, stat_ref) = refs[:4], refs[4:]
    by_core(lambda q, g: part(2, q, g, key_ref, value_ref, s_in, s_ref, dw_ref), planes)
    for k in range(4):
        s = s_ref[k] * SCALE + jnp.dot(hot_ref[...], table_ref[k], preferred_element_type=F32)
        top = jnp.max(s, axis=0, keepdims=True)
        e = jnp.where(s > -1e29, jnp.exp(s - top), 0.0)
        s_ref[k] = e
        total = jnp.sum(e, axis=0, keepdims=True)
        for to in range(16):
            stat_ref[to, k : k + 1, :] = top
            stat_ref[to, 4 + k : 5 + k, :] = total


def delta_kernel(e_ref, dw_ref, stat_ref, all_ref, delta_ref, factor_ref):
    tops = all_ref[:, 0:4, :]
    peak = jnp.max(tops, axis=0)
    whole = jnp.sum(all_ref[:, 4:8, :] * jnp.exp(tops - peak[None]), axis=0)
    factor_ref[...] = jnp.exp(stat_ref[0, 0:4, :] - peak) / whole

    def body(k, _):
        low = (e_ref[k] * factor_ref[pl.ds(k, 1), :]).astype(BF16).astype(F32)
        delta = jnp.sum(low * dw_ref[k], axis=0, keepdims=True)
        for to in range(16):
            delta_ref[to, pl.ds(k, 1), :] = delta
        return 0

    lax.fori_loop(0, 4, body, 0)


def own_rows(values_ref, other):
    y, zhi = lax.axis_index("y"), lax.axis_index("zhi")
    lanes = pl.ds(pl.multiple_of(lax.div(zhi, 2) * 128, 128), 128)
    both = lax.dot_general(values_ref[y, :, lanes], other, TN, preferred_element_type=F32)
    return jnp.where(lax.rem(zhi, 2) == 1, both[ROWS:], both[:ROWS])


def back_kernel(*refs):
    planes, refs = refs[:16], refs[16:]
    e_ref, dw_ref, factor_ref, deltas_ref, key_ref, value_ref, keep_ref, give_ref, gk_ref, gv_ref = refs[:10]
    low_ref, ds_ref, qm_ref, gm_ref = refs[10:]
    core, x_now = lax.axis_index("core"), lax.axis_index("x")
    delta = jnp.sum(deltas_ref[...], axis=0)
    for k in range(4):
        w = e_ref[k] * factor_ref[k : k + 1, :]
        low_ref[k] = w.astype(BF16)
        ds_ref[k] = (w * (dw_ref[k] - delta[k : k + 1, :])).astype(BF16)
    for x in range(4):
        mixed = own_rows(low_ref, value_ref[x])
        grads = own_rows(ds_ref, key_ref[x]) * SCALE
        both = jnp.concatenate([mixed, grads], axis=0).T
        for zlo in range(2):
            low, high = both[zlo * 192 : zlo * 192 + FEAT], both[zlo * 192 + FEAT : zlo * 192 + 192]
            keep_ref[zlo * 4 + x] = jnp.where(core == 0, low, high)
            give_ref[zlo * 4 + x] = jnp.where(core == 0, high, low)

    mine = lax.axis_index(LATENT)
    rows = pl.ds(pl.multiple_of((lax.div(mine, 8) * 2 + lax.rem(mine, 2)) * FEAT, 32), FEAT)
    back = lax.rem(x_now + 4 - lax.rem(lax.div(mine, 2), 4), 4)
    for side in range(2):
        for step in range(4):
            pair = planes[step * 4 + side * 2 : step * 4 + side * 2 + 2]

            def take_q(pair=pair):
                for k in range(4):
                    qm_ref[place(k)[1]] = pair[k // 2][k % 2, rows, :]

            def take_g(pair=pair, step=step):
                for half in range(2):

                    def take(half=half):
                        gm_ref[place(step)[1]] = pair[half][lax.rem(back, 2), rows, :]

                    pl.when(lax.div(back, 2) == half)(take)

            pl.when((core == side) & (back == step))(take_q)
            pl.when(core != side)(take_g)
    gk = jnp.zeros((FEAT, TILES), F32)
    gv = jnp.zeros((FEAT, TILES), F32)
    for k in range(4):
        gk = gk + lax.dot_general(qm_ref[k], ds_ref[k], NT, preferred_element_type=F32)
        gv = gv + lax.dot_general(gm_ref[k], low_ref[k], NT, preferred_element_type=F32)
    gk_ref[...] = (gk * SCALE).astype(BF16)
    gv_ref[...] = gv.astype(BF16)


def last_kernel(terms_ref, attended_ref, gq_ref):
    both = jnp.sum(terms_ref[...], axis=0).T
    attended_ref[...] = both[:ROWS].astype(BF16)
    gq_ref[...] = both[ROWS:].astype(BF16)


def call(kernel, outs, ins, args, scratch=(), flops=0, moved=0, limit=16, aliases=None):
    vmem = pl.BlockSpec(memory_space=pltpu.VMEM)
    specs = {"v": vmem, "V": vmem, "H": pl.BlockSpec(memory_space=pl.ANY), "a": pl.BlockSpec(memory_space=pl.ANY)}
    pins = {"V": pltpu.VMEM, "H": pltpu.HBM}
    shapes = [pltpu.VMEM(shape, kind) if c == "V" else jax.ShapeDtypeStruct(shape, kind) for c, shape, kind in outs]
    args = [pltpu.with_memory_space_constraint(a, pins[c]) if c in pins else a for c, a in zip(ins, args)]
    return pl.pallas_call(
        kernel,
        out_shape=shapes,
        in_specs=[specs[c] for c in ins],
        out_specs=[vmem] * len(outs),
        scratch_shapes=list(scratch),
        input_output_aliases=aliases or {},
        compiler_params=pltpu.CompilerParams(vmem_limit_bytes=limit * MIB),
        cost_estimate=pl.CostEstimate(flops=flops, bytes_accessed=moved, transcendentals=0),
    )(*args)


PLANE = [(x, core, y) for x in range(4) for core in range(2) for y in range(4)]


def along(value, stage, step):
    pairs = []
    for i, (x, core, y) in enumerate(PLANE):
        to = (x, core, (y + step) % 4) if core == stage else ((x + step) % 4, core, y)
        pairs.append((i, PLANE.index(to)))
    return lax.ppermute(value, ("x", "core", "y"), pairs)


def swap(value):
    return lax.ppermute(value, "core", [(0, 1), (1, 0)])


def shards(queries, tile_keys, tile_values, region_ids, block_list, region_bias, grad_out):
    dma = pltpu.SemaphoreType.DMA
    wide = (4, TILES, WIDE)
    sides = (4, TILES, PART)

    (packed,) = call(
        pack_kernel,
        [("v", (16, 80, 128), BF16)],
        "HHHH",
        (block_list, region_bias, queries, grad_out),
        [
            pltpu.SMEM(block_list.shape, jnp.int32),
            pltpu.SMEM(region_bias.shape, F32),
            pltpu.VMEM((ROWS, FEAT), BF16),
            pltpu.VMEM((ROWS, FEAT), BF16),
            dma((4,)),
        ],
    )
    got = lax.all_to_all(packed, ("zhi", "zlo", "core"), 0, 0)
    keys, values, hot = call(
        prepare_kernel,
        [("V", sides, BF16), ("V", sides, BF16), ("V", (TILES, 256), BF16)],
        "HHv",
        (tile_keys, tile_values, region_ids.reshape(1, TILES)),
        [pltpu.VMEM((TILES, D), BF16), pltpu.VMEM((TILES, D), BF16), dma((2,))],
        0,
        10_000_000,
    )
    (block,) = call(turn_kernel, [("v", (HIGH, WIDE), BF16)], "v", (got,))
    half = (2, HIGH, WIDE)
    line = call(
        stack_kernel,
        [("v", half, BF16)] * 2,
        "vvvva",
        [block, *(along(block, 0, k) for k in (1, 2, 3)), hot],
    )
    up = [along(piece, 1, 1) for piece in line]
    down = [along(piece, 1, 3) for piece in line]
    flops = 4 * TILES * 256 * D
    moved = 8_000_000
    planes = [[*line, *(swap(piece) for piece in line)]]
    s, dw, table = call(
        first_kernel,
        [("V", wide, F32), ("V", wide, F32), ("V", (4, 256, WIDE), BF16)],
        "vvvvVV",
        (*planes[0], keys, values),
        (),
        flops,
        moved,
    )
    up[0], down[1] = call(tie_kernel, [("V", half, BF16)] * 2, "VVa", (up[0], down[1], s), aliases={0: 0, 1: 1})
    across = [along(up[0], 1, 1), along(down[1], 1, 3)]
    for step, pair in ((1, up), (3, down)):
        planes.append([*pair, *(swap(piece) for piece in pair)])
        s, dw = call(
            functools.partial(middle_kernel, step),
            [("V", wide, F32), ("V", wide, F32)],
            "vvvvVVVV",
            (*planes[-1], keys, values, s, dw),
            (),
            flops,
            moved,
            aliases={6: 0, 7: 1},
        )
    across = call(tie_kernel, [("V", half, BF16)] * 2, "VVa", (*across, s), aliases={0: 0, 1: 1})
    planes.insert(2, [*across, *(swap(piece) for piece in across)])
    e, dw, stat = call(
        end_kernel,
        [("V", wide, F32), ("V", wide, F32), ("v", (16, 8, WIDE), F32)],
        "vvvvVVVVVV",
        (*planes[2], keys, values, table, hot, s, dw),
        (),
        flops,
        moved,
        aliases={8: 0, 9: 1},
    )
    stats = lax.all_to_all(stat, PATCH, 0, 0)
    delta, factor = call(
        delta_kernel,
        [("v", (16, 4, WIDE), F32), ("V", (4, WIDE), F32)],
        "VVvv",
        (e, dw, stat, stats),
        (),
        4 * TILES * 1024,
        8_000_000,
    )
    deltas = lax.all_to_all(delta, PATCH, 0, 0)
    eighth = (8, FEAT, 128)
    keep, give, grad_keys, grad_values = call(
        back_kernel,
        [("V", eighth, F32), ("v", eighth, F32), ("v", (FEAT, TILES), BF16), ("v", (FEAT, TILES), BF16)],
        "v" * 16 + "VVVvVV",
        (*planes[0], *planes[1], *planes[2], *planes[3], e, dw, factor, deltas, keys, values),
        [pltpu.VMEM(wide, BF16), pltpu.VMEM(wide, BF16), pltpu.VMEM((4, FEAT, WIDE), BF16), pltpu.VMEM((4, FEAT, WIDE), BF16)],
        4 * TILES * 1024 * FEAT,
        10_000_000,
    )
    (chip,) = call(add_kernel, [("v", eighth, F32)], "Vv", (keep, swap(give)))
    sums = lax.all_to_all(chip, ("zlo", "x"), 0, 0)
    attended, grad_queries = call(last_kernel, [("v", (ROWS, FEAT), BF16)] * 2, "v", (sums,))
    return (attended, grad_queries, grad_keys, grad_values)


def solution(mesh):
    fine = Mesh(mesh.devices.reshape(2, 4, 2, 4, 4), PATCH + LATENT)
    in_specs = (
        P(LATENT, PATCH),
        P(PATCH, None),
        P(PATCH, None),
        P(PATCH),
        P(LATENT, None),
        P(LATENT, None),
        P(LATENT, PATCH),
    )
    out_specs = (P(LATENT, PATCH),) * 4
    return jax.shard_map(shards, mesh=fine, in_specs=in_specs, out_specs=out_specs, check_vma=False)
```

```python
import functools

import jax
import jax.numpy as jnp
from jax import lax
from jax.experimental import pallas as pl
from jax.experimental.pallas import tpu as pltpu
from jax.sharding import Mesh, PartitionSpec as P

BLOCK = 128
D = 1536
TILES = 768
ROWS = 64
FEAT = 96
NB = 6
WIDE = 256
PART = 384
SENT = 200
PATCH = ("zlo", "x", "core")
LATENT = ("zhi", "y")
SCALE = D ** (-0.5)
F32 = jnp.float32
BF16 = jnp.bfloat16
NT = (((1,), (1,)), ((), ()))
TN = (((0,), (0,)), ((), ()))
MIB = 1024 * 1024


def iota(shape, dim):
    return lax.broadcasted_iota(jnp.int32, shape, dim)


def pack_kernel(list_ref, bias_ref, q_ref, g_ref, out_ref, list_s, bias_s, q_v, g_v, sems):
    copies = [
        pltpu.make_async_copy(src, dst, sems.at[i])
        for i, (src, dst) in enumerate(((list_ref, list_s), (bias_ref, bias_s), (q_ref, q_v), (g_ref, g_v)))
    ]
    for copy in copies:
        copy.start()
    for copy in copies:
        copy.wait()
    lane = iota((1, 128), 1)
    mask = jnp.zeros((1, 128), F32)
    for i in range(list_ref.shape[1]):
        mask = jnp.where(lane == list_s[0, i], 1.0, mask)
    bias = jnp.zeros((1, 128), F32)
    for i in range(16):
        bias = jnp.where(lane == i, bias_s[0, i], bias)
    high = bias.astype(BF16).astype(F32)
    middle = (bias - high).astype(BF16).astype(F32)
    last = bias - high - middle
    kind = iota((16, 128), 0) % 4
    meta = jnp.where(kind == 0, mask, jnp.where(kind == 1, high, jnp.where(kind == 2, middle, last)))
    meta = meta.astype(BF16)
    for core, ref in ((0, q_v), (1, g_v)):
        tail = ref[48:64, :]
        side = jnp.concatenate([tail[:, 0:32], tail[:, 32:64], tail[:, 64:96]], axis=0)
        rows = jnp.concatenate([ref[0:48, :], side], axis=1)
        for to in range(core, 16, 2):
            out_ref[to, 0:48, :] = rows
            out_ref[to, 48:64, :] = meta


def turn_kernel(got_ref, out_ref, meta_ref):
    def opened(at):
        side = got_ref[at, 0:48, 96:128]
        tail = jnp.concatenate([side[0:16], side[16:32], side[32:48]], axis=1)
        return [got_ref[at, 0:48, 0:96], tail]

    for part in range(4):
        for pair in range(2):
            both = jnp.concatenate(opened(pair * 8 + part) + opened(pair * 8 + 4 + part), axis=0)
            out_ref[part * FEAT : part * FEAT + FEAT, pair * 128 : pair * 128 + 128] = both.T
    owner = iota((16, 128), 0) // 4
    meta = jnp.zeros((16, 128), F32)
    for zhi in range(4):
        meta = jnp.where(owner == zhi, got_ref[zhi * 4, 48:64, :].astype(F32), meta)
    meta_ref[...] = meta


def tie_kernel(*refs):
    pass


def prepare_kernel(key_ref, value_ref, region_ref, key_out, value_out, hot_ref, key_v, value_v, sems):
    copies = [
        pltpu.make_async_copy(key_ref, key_v, sems.at[0]),
        pltpu.make_async_copy(value_ref, value_v, sems.at[1]),
    ]
    for copy in copies:
        copy.start()
    for block in range(NB):
        label = iota((256, BLOCK), 0)
        region = region_ref[:, block * BLOCK : (block + 1) * BLOCK]
        at = lax.axis_index(PATCH) * NB + block
        hot = (label == at) | ((label >= 96) & (label < 144) & (label % 16 == region))
        hot_ref[block * BLOCK : (block + 1) * BLOCK, :] = jnp.where(hot, 1.0, 0.0).T.astype(BF16)
    for copy, src, dst in zip(copies, (key_v, value_v), (key_out, value_out)):
        copy.wait()
        for x in range(4):
            low = src[:, x * 192 : x * 192 + 192]
            high = src[:, (4 + x) * 192 : (4 + x) * 192 + 192]
            dst[x] = jnp.concatenate([low, high], axis=1)


def x_back(back):
    return lax.rem(lax.axis_index("x") + 4 - back, 4)


def products(table_ref, planes):
    total = jnp.zeros((TILES, WIDE), F32)
    for k in range(4):
        total = total + jnp.dot(table_ref[x_back(k)], planes[k][...], preferred_element_type=F32)
    return total


def own_slices(planes, out_ref):
    zhi = lax.axis_index("zhi")
    rows = pl.ds(pl.multiple_of(lax.div(zhi, 2) * 192, 64), 192)
    for half in range(2):
        back = lax.rem(lax.axis_index("x") + 4 - lax.rem(zhi, 2) * 2 - half, 4)
        for k in range(4):

            def take(k=k, half=half):
                out_ref[half] = planes[k][rows, :]

            pl.when(back == k)(take)


def near_kernel(*refs):
    planes, (key_ref, value_ref, acc_ref, mine_ref) = refs[:4], refs[4:]
    own_slices(planes, mine_ref)
    core = lax.axis_index("core")

    def work(table_ref):
        acc_ref[...] = products(table_ref, planes)

    pl.when(core == 0)(lambda: work(key_ref))
    pl.when(core == 1)(lambda: work(value_ref))


def far_kernel(*refs):
    planes, refs = refs[:4], refs[4:]
    key_ref, value_ref, hot_ref, meta_ref, acc_ref, mine_ref, e_ref, dw_ref, stat_ref, far_ref = refs
    own_slices(planes, far_ref)
    group = iota((1, WIDE), 1) // ROWS
    meta = meta_ref[...].T
    parts = []
    for kind in range(4):
        height = 96 if kind == 0 else 16
        piece = jnp.zeros((height, WIDE), F32)
        for zhi in range(4):
            piece = jnp.where(group == zhi, meta[:height, zhi * 4 + kind : zhi * 4 + kind + 1], piece)
        parts.append((piece - 1.0) * 1e30 if kind == 0 else piece)
    table = jnp.concatenate(parts + [jnp.zeros((112, WIDE), F32)], axis=0).astype(BF16)
    core = lax.axis_index("core")

    def work(table_ref, old_ref, new_ref):
        old_ref[...] = acc_ref[...]
        new_ref[...] = products(table_ref, planes)

    pl.when(core == 0)(lambda: work(value_ref, e_ref, dw_ref))
    pl.when(core == 1)(lambda: work(key_ref, dw_ref, e_ref))
    s = e_ref[...] * SCALE + jnp.dot(hot_ref[...], table, preferred_element_type=F32)
    top = jnp.max(s, axis=0, keepdims=True)
    e = jnp.where(s > -1e29, jnp.exp(s - top), 0.0)
    e_ref[...] = e
    dw = dw_ref[...]

    def down(value):
        return jnp.sum(value, axis=0, keepdims=True)

    first = jnp.max(e, axis=0, keepdims=True)
    second = jnp.max(jnp.where(e == first, 0.0, e), axis=0, keepdims=True)
    first_dw = down(jnp.where(e == first, dw, 0.0))
    second_dw = down(jnp.where(e == second, dw, 0.0))
    sent = [top, down(e), down(e * dw), first, first_dw, second, second_dw]
    for to in range(16):
        for i in range(7):
            stat_ref[to, i : i + 1, :] = sent[i]


def y_terms(mine_ref, weights_ref, terms_ref, which, own_ref, outs, scale):
    for half in range(2):
        both = lax.dot_general(mine_ref[half], weights_ref[...], NT, preferred_element_type=F32) * scale
        terms_ref[half * 2] = both[:FEAT]
        terms_ref[half * 2 + 1] = both[FEAT:]
    own_ref[which] = terms_ref[lax.axis_index("y")]
    largest = jnp.max(jnp.max(jnp.abs(terms_ref[...]), axis=0), axis=0, keepdims=True)
    largest = jnp.maximum(jnp.max(largest, axis=1, keepdims=True), 1e-30)
    exponent = jnp.ceil(jnp.log2(largest)) - 15.0
    factor = jnp.exp2(-exponent)
    for k in range(3):
        outs[k][which * FEAT : which * FEAT + FEAT, :] = terms_ref[lax.rem(lax.axis_index("y") + k + 1, 4)] * factor
    return exponent


def term_kernel(e_ref, dw_ref, stat_ref, all_ref, near_ref, far_ref, low_ref, ds_ref, *refs):
    tops, totals, products_, one, one_dw, two, two_dw = [all_ref[:, i, :] for i in range(7)]
    peak = jnp.max(tops, axis=0, keepdims=True)
    scale = jnp.exp(tops - peak)
    whole = jnp.sum(totals * scale, axis=0, keepdims=True)
    scale = scale / whole

    def rounding(value):
        weight = value * scale
        return weight.astype(BF16).astype(F32) - weight

    delta = products_ * scale + rounding(one) * one_dw + rounding(two) * two_dw
    delta = jnp.sum(delta, axis=0, keepdims=True)
    factor = jnp.exp(stat_ref[0, 0:1, :] - peak) / whole
    w = e_ref[...] * factor
    low_ref[...] = w.astype(BF16)
    ds_ref[...] = (w * (dw_ref[...] - delta)).astype(BF16)
    core = lax.axis_index("core")
    for i in range(2):
        refs[5][i] = jnp.where(core == 0, near_ref[i], far_ref[i])
        refs[6][i] = jnp.where(core == 0, far_ref[i], near_ref[i])
    first = y_terms(refs[5], ds_ref, refs[4], 0, refs[0], refs[1:4], SCALE)
    second = y_terms(refs[6], low_ref, refs[4], 1, refs[0], refs[1:4], 1.0)
    row = iota((8, TILES), 0)
    for k in range(3):
        refs[k + 1][2 * FEAT : SENT, :] = jnp.where(row == 0, first, jnp.where(row == 1, second, 0.0))


def own_rows(values_ref):
    zhi = lax.axis_index("zhi")
    lanes = pl.ds(pl.multiple_of(lax.div(zhi, 2) * 128, 128), 128)
    both = values_ref[:, lanes].T
    return jnp.where(lax.rem(zhi, 2) == 1, both[ROWS:], both[:ROWS])


def row_kernel(low_ref, ds_ref, key_ref, value_ref, keep_ref, give_ref):
    first = lax.axis_index("core") == 0
    own_low, own_ds = own_rows(low_ref), own_rows(ds_ref)
    for x in range(4):
        mixed = jnp.dot(own_low, value_ref[x], preferred_element_type=F32)
        grads = jnp.dot(own_ds, key_ref[x], preferred_element_type=F32) * SCALE
        both = jnp.concatenate([mixed, grads], axis=0).T
        for zlo in range(2):
            low, high = both[zlo * 192 : zlo * 192 + FEAT], both[zlo * 192 + FEAT : zlo * 192 + 192]
            keep_ref[zlo * 4 + x] = jnp.where(first, low, high)
            give_ref[zlo * 4 + x] = jnp.where(first, high, low)


def halve_kernel(keep_ref, got_ref, next_keep, next_give):
    zlo = lax.axis_index("zlo")
    for i in range(4):
        kept, given = zlo * 4 + i, 4 - zlo * 4 + i
        next_keep[i] = keep_ref[kept] + got_ref[kept]
        next_give[i] = keep_ref[given] + got_ref[given]


def quarter_kernel(keep_ref, got_ref, *outs):
    for k in range(4):
        at = lax.rem(lax.axis_index("x") + k, 4)
        outs[k][...] = keep_ref[at] + got_ref[at]


def last_kernel(own_ref, a_ref, b_ref, c_ref, *refs):
    rows, (attended_ref, gq_ref, gk_ref, gv_ref) = refs[:4], refs[4:]
    for which, out_ref in ((0, gk_ref), (1, gv_ref)):
        total = own_ref[which]
        for ref in (a_ref, b_ref, c_ref):
            scale = jnp.exp2(ref[2 * FEAT + which : 2 * FEAT + which + 1, :])
            total = total + ref[which * FEAT : which * FEAT + FEAT, :] * scale
        out_ref[...] = total.astype(BF16)
    both = (rows[0][...] + rows[1][...] + rows[2][...] + rows[3][...]).T
    attended_ref[...] = both[:ROWS].astype(BF16)
    gq_ref[...] = both[ROWS:].astype(BF16)


def call(kernel, outs, ins, args, scratch=(), flops=0, moved=0, limit=16, aliases=None):
    vmem = pl.BlockSpec(memory_space=pltpu.VMEM)
    specs = {"v": vmem, "V": vmem, "H": pl.BlockSpec(memory_space=pl.ANY), "a": pl.BlockSpec(memory_space=pl.ANY)}
    pins = {"V": pltpu.VMEM, "H": pltpu.HBM}
    shapes = [pltpu.VMEM(shape, kind) if c == "V" else jax.ShapeDtypeStruct(shape, kind) for c, shape, kind in outs]
    args = [pltpu.with_memory_space_constraint(a, pins[c]) if c in pins else a for c, a in zip(ins, args)]
    return pl.pallas_call(
        kernel,
        out_shape=shapes,
        in_specs=[specs[c] for c in ins],
        out_specs=[vmem] * len(outs),
        scratch_shapes=list(scratch),
        input_output_aliases=aliases or {},
        compiler_params=pltpu.CompilerParams(vmem_limit_bytes=limit * MIB),
        cost_estimate=pl.CostEstimate(flops=flops, bytes_accessed=moved, transcendentals=0),
    )(*args)


MOVES = [[(i, (i + k) % 4) for i in range(4)] for k in (1, 2, 3)]


def ring(value, axis):
    return [lax.ppermute(value, axis, move) for move in MOVES]


def swap(value):
    return lax.ppermute(value, "core", [(0, 1), (1, 0)])


def tie(arrays, after):
    outs = [("V", array.shape, array.dtype) for array in arrays]
    ins = "V" * len(arrays) + "a" * len(after)
    return call(tie_kernel, outs, ins, (*arrays, *after), aliases={i: i for i in range(len(arrays))})


def y_sends(terms):
    sent = [lax.ppermute(value.astype(jnp.float16), "y", move).astype(F32) for value, move in zip(terms, MOVES)]
    return [sent[i] for i in (0, 2, 1)]


def shards(queries, tile_keys, tile_values, region_ids, block_list, region_bias, grad_out):
    dma = pltpu.SemaphoreType.DMA
    wide = (TILES, WIDE)
    sides = (4, TILES, PART)
    flops = 2 * TILES * WIDE * D

    (packed,) = call(
        pack_kernel,
        [("v", (16, 64, 128), BF16)],
        "HHHH",
        (block_list, region_bias, queries, grad_out),
        [
            pltpu.SMEM(block_list.shape, jnp.int32),
            pltpu.SMEM(region_bias.shape, F32),
            pltpu.VMEM((ROWS, FEAT), BF16),
            pltpu.VMEM((ROWS, FEAT), BF16),
            dma((4,)),
        ],
    )
    got = lax.all_to_all(packed, ("zhi", "zlo", "core"), 0, 0)
    keys, values, hot = call(
        prepare_kernel,
        [("V", sides, BF16), ("V", sides, BF16), ("V", (TILES, 256), BF16)],
        "HHv",
        (tile_keys, tile_values, region_ids.reshape(1, TILES)),
        [pltpu.VMEM((TILES, D), BF16), pltpu.VMEM((TILES, D), BF16), dma((2,))],
        flops,
        10_000_000,
    )
    block, meta = call(turn_kernel, [("V", (PART, WIDE), BF16), ("V", (16, 128), F32)], "v", (got,))
    near = [block, *ring(block, "x")]
    (near[3],) = tie([near[3]], [hot])
    far = [swap(plane) for plane in near]

    slices = (2, 192, WIDE)
    term = (2, FEAT, TILES)
    acc, near_mine = call(
        near_kernel,
        [("V", wide, F32), ("V", slices, BF16)],
        "v" * 4 + "VV",
        (*near, keys, values),
        (),
        flops,
        5_000_000,
    )
    e, dw, stat, far_mine = call(
        far_kernel,
        [("V", wide, F32), ("V", wide, F32), ("v", (16, 7, WIDE), F32), ("V", slices, BF16)],
        "v" * 4 + "VVVVVV",
        (*far, keys, values, hot, meta, acc, near_mine),
        (),
        flops,
        5_000_000,
    )
    stats = lax.all_to_all(stat, PATCH, 0, 0)
    low, ds, own, *terms = call(
        term_kernel,
        [("V", wide, BF16), ("V", wide, BF16), ("V", (2, FEAT, TILES), F32)] + [("V", (SENT, TILES), F32)] * 3,
        "VVvvVV",
        (e, dw, stat, stats, near_mine, far_mine),
        [pltpu.VMEM((4, FEAT, TILES), F32), pltpu.VMEM(slices, BF16), pltpu.VMEM(slices, BF16)],
        flops // 2,
        8_000_000,
    )
    terms = y_sends(terms)
    keep, give = call(
        row_kernel,
        [("V", (8, FEAT, 128), F32), ("V", (8, FEAT, 128), F32)],
        "VVVV",
        (low, ds, keys, values),
        (),
        flops // 4,
        4_000_000,
    )
    half = ("V", (4, FEAT, 128), F32)
    keep, give = call(halve_kernel, [half, half], "VV", (keep, swap(give)))
    got = lax.ppermute(give, "zlo", [(0, 1), (1, 0)])
    rows = call(quarter_kernel, [("V", (FEAT, 128), F32)] * 4, "VV", (keep, got))
    rows = [rows[0]] + [lax.ppermute(value, "x", move) for value, move in zip(rows[1:], MOVES)]
    attended, grad_queries, grad_keys, grad_values = call(
        last_kernel,
        [("v", (ROWS, FEAT), BF16)] * 2 + [("v", (FEAT, TILES), BF16)] * 2,
        "VvvvVVVV",
        (own, *terms, *rows),
    )
    return (attended, grad_queries, grad_keys, grad_values)


def solution(mesh):
    fine = Mesh(mesh.devices.reshape(2, 4, 2, 4, 4), PATCH + LATENT)
    in_specs = (
        P(LATENT, PATCH),
        P(PATCH, None),
        P(PATCH, None),
        P(PATCH),
        P(LATENT, None),
        P(LATENT, None),
        P(LATENT, PATCH),
    )
    out_specs = (P(LATENT, PATCH),) * 4
    return jax.shard_map(shards, mesh=fine, in_specs=in_specs, out_specs=out_specs, check_vma=False)
```
